32 devices in a mesh: groups: 2 (over y), aux: 4 (over z), row: 4 (over x, core).
Axes of the slice: x: 2, y: 2, z: 4, core: 2. Of those that a mesh axis runs over, the one named last changes fastest.
Arguments:
- tensor_tiles: bfloat16 [64, 96, 128, 128], P(('groups', 'aux'), 'row'), parts along dimension 0, may hold values from -6 to 6
- pair_rows: int32 [8, 96], P(('groups', 'aux'), 'row'), parts along dimension 0, may hold values from 0 to 15, as said below
- pair_cols: int32 [8, 96], P(('groups', 'aux'), 'row'), parts along dimension 0, may hold values from 0 to 63
- live_count: int32 [8, 4], P(('groups', 'aux'), 'row'), parts along dimension 0, may hold values from 16 to 24, as said below
- orbitals: bfloat16 [8192, 512], P(None, 'groups'), parts along dimension 1, may hold values from -0.375 to 0.375
- metric: bfloat16 [32, 32], replicated, as said below
Outputs:
- exchange: float32 [1024, 8192], P(('groups', 'aux'), 'row'), parts along dimension 0
The draws below stay inside these ranges and needn't reach their ends.
There are 2 independent parts, one for each index of `groups`. The reference program is written for one: setup_inputs(seed, part) draws one part's arguments, and reference() takes and returns one part's arrays. A program takes and returns all parts, laid end to end along the dimension named above; an argument that names none is the same for every part. Nothing has to cross between parts.
Inputs may be any that keep to these rules, and one draw needn't show every extreme that they name: `pair_rows`: slot t < 16 of every device holds p shell block t. `live_count`: some device has all 24 slots live. `metric`: symmetric.
All inputs are finite; a program needn't handle non-finite values.
Results may differ from the reference program's by a relative error of at most 0.0043.
Values may be sent and summed in bfloat16 or wider, within the bound.
No kernel may reach another device: no remote copies, remote signals or barrier semaphores. Data moves between devices by JAX's collectives and lax.ppermute only.
A program may use at most 128 MiB of HBM per device.

```python
import jax
import jax.numpy as jnp
from jax import lax

NBF = 8192
SB = 128
NOCC = 256
AUX_DEV = 8
NT = 24
KR = 128
NAUX = 32
KROWS = 512
NSB = 64
N_AUX = 4
N_ROW = 4


def pattern_draw(key):
    per_row = NBF // (SB * N_ROW)
    first_key, second_key, third_key, fourth_key = jax.random.split(key, 4)
    slot_ids = jnp.arange(N_ROW * NT, dtype=jnp.int32) % NT
    owners = jnp.arange(N_ROW * NT, dtype=jnp.int32) // NT
    extras = jax.random.randint(first_key, (N_AUX, N_ROW * NT), 0, per_row)
    row_ids = jnp.where(slot_ids[None, :] < per_row, slot_ids[None, :], extras).astype(jnp.int32)
    offsets = jax.random.randint(second_key, (N_AUX, N_ROW * NT), -3, 4)
    col_ids = jnp.mod(owners[None, :] * per_row + row_ids + offsets, NSB).astype(jnp.int32)
    counts = jax.random.randint(third_key, (N_AUX, N_ROW), per_row, NT + 1)
    fullest = jax.random.randint(fourth_key, (), 0, N_AUX * N_ROW)
    places = jnp.arange(N_AUX * N_ROW, dtype=jnp.int32).reshape(N_AUX, N_ROW)
    counts = jnp.where(places == fullest, NT, counts).astype(jnp.int32)
    return (row_ids, col_ids, counts)


def draw_pair_rows(key, part):
    return pattern_draw(key)[0]


def draw_pair_cols(key, part):
    return pattern_draw(key)[1]


def draw_live_count(key, part):
    return pattern_draw(key)[2]


def draw_metric(key, part):
    key = jax.random.fold_in(key, 7)
    first_key, second_key = jax.random.split(key, 2)
    noises = jax.random.normal(first_key, (NAUX, NAUX), jnp.float32)
    diagonal = jax.random.uniform(second_key, (NAUX,), jnp.float32, 0.5, 1.5)
    mixed = 0.5 * (noises + noises.T) * (0.6 / NAUX ** 0.5) + jnp.diag(diagonal)
    return (mixed * (NAUX * NOCC) ** (-0.25)).astype(jnp.bfloat16)


def level_of(own_key, extent, shards, smallest, high):
    def one(dim, shards_of):
        steps = jax.random.uniform(jax.random.fold_in(jax.random.fold_in(own_key, 6), dim), (shards_of,), jnp.float32, smallest / len(shards), high / len(shards))
        return jnp.repeat(jnp.exp(steps), extent[dim] // shards_of).reshape((-1,) + (1,) * (len(extent) - dim - 1))

    gain = one(*shards[0])
    for cut in shards[1:]:
        gain = gain * one(*cut)
    return gain


def normal_values(own_key, shape, spread, bound, pieces=(), held_as=jnp.bfloat16):
    values = jax.random.normal(own_key, shape, jnp.float32) * spread
    if len(pieces) > 0:
        values = level_of(own_key, shape, pieces, -0.22, 0.18) * values
    return jnp.clip(values, min=-bound, max=bound).astype(held_as)


def setup_inputs(seed: int = 0, part: int = 0) -> dict:
    key_list = jax.random.split(jax.random.key(seed), 7)
    part_splits = jax.random.split(jax.random.fold_in(key_list[6], part), 7)
    return {
        "tensor_tiles": normal_values(part_splits[0], (NAUX, N_ROW * NT, SB, SB), 1.0, 6.0, ((0, 4), (1, 4))),
        "pair_rows": draw_pair_rows(jax.random.fold_in(jax.random.fold_in(key_list[6], part), 71), part),
        "pair_cols": draw_pair_cols(jax.random.fold_in(jax.random.fold_in(key_list[6], part), 71), part),
        "live_count": draw_live_count(jax.random.fold_in(jax.random.fold_in(key_list[6], part), 71), part),
        "orbitals": normal_values(part_splits[4], (NBF, NOCC), (2 * SB) ** -0.5, 0.375),
        "metric": draw_metric(jax.random.fold_in(key_list[6], 71), part),
    }


def reference(tensor_tiles, pair_rows, pair_cols, live_count, orbitals, metric):
    rows_dev = NBF // N_ROW
    blocks_dev = rows_dev // SB
    slot_ids = jnp.arange(N_ROW * NT, dtype=jnp.int32) % NT
    owners = jnp.arange(N_ROW * NT, dtype=jnp.int32) // NT
    orbital_blocks = orbitals.reshape(NSB, SB, NOCC).astype(jnp.float32)
    shaped = tensor_tiles.reshape(N_AUX, AUX_DEV, N_ROW * NT, SB, SB)

    def one_shard(inputs):
        shard_tiles, row_ids, col_ids, counts_dev = inputs
        column_rows = orbital_blocks[col_ids]
        partial_value = jnp.einsum('qtps,tsi->tqip', shard_tiles.astype(jnp.float32), column_rows,
                             precision=lax.Precision.HIGHEST)
        active = slot_ids < counts_dev[owners]
        target = owners * blocks_dev + row_ids
        placing = ((target[:, None] == jnp.arange(N_ROW * blocks_dev, dtype=jnp.int32)[None, :])
                   & active[:, None]).astype(jnp.float32)
        summed = jnp.einsum('tb,tqip->qibp', placing, partial_value, precision=lax.Precision.HIGHEST)
        return summed.reshape(AUX_DEV, NOCC, NBF).astype(jnp.bfloat16)

    halves = lax.map(one_shard, (shaped, pair_rows, pair_cols, live_count))
    half_tensor = halves.reshape(NAUX, NOCC * NBF)
    fitted = jnp.dot(metric, half_tensor, preferred_element_type=jnp.float32).astype(jnp.bfloat16)
    window = fitted.reshape(NAUX, NOCC, N_ROW, rows_dev)[:, :, :, :KR].reshape(NAUX * NOCC, KROWS)
    return jnp.dot(window.T, fitted.reshape(NAUX * NOCC, NBF), preferred_element_type=jnp.float32)
```

```python
import functools

import jax
import jax.numpy as jnp
from jax import lax
from jax.experimental import pallas as pl
from jax.experimental.pallas import tpu as pltpu
from jax.sharding import PartitionSpec as P

KR = 128
HALVES = 2
LIMIT = 48 * 1024 * 1024
F32 = jnp.float32
BF16 = jnp.bfloat16


def half_body(first, blocks, extras, outs, rows, cols, live, tile, more, orb, *rest):
    orbs, out_refs, acc = rest[:extras], rest[extras:extras + outs], rest[-1]
    aux_dev, _, width, _ = tile.shape
    occ = orb.shape[1]
    block = pl.program_id(0) + first
    for q in range(aux_dev):
        acc[:, q * occ:(q + 1) * occ] = jnp.dot(tile[q, 0], orb[...], preferred_element_type=F32)
    for e in range(extras):
        @pl.when((rows[blocks + e] == block) & (blocks + e < live[0]))
        def _():
            for q in range(aux_dev):
                acc[:, q * occ:(q + 1) * occ] += jnp.dot(
                    more[q, e], orbs[e][...], preferred_element_type=F32)
    part = width // outs
    for k in range(outs):
        out_refs[k][...] = acc[k * part:(k + 1) * part, :].astype(BF16)


def half_rows(tiles, rows, cols, live, orbitals, first, count, outs):
    aux_dev, slots, width, _ = tiles.shape
    basis, occ = orbitals.shape
    blocks = basis // (width * lax.axis_size("row"))
    extras = slots - blocks
    wide = aux_dev * occ
    in_specs = [
        pl.BlockSpec((aux_dev, 1, width, width), lambda b, r, c, n: (0, b + first, 0, 0)),
        pl.BlockSpec((aux_dev, extras, width, width), lambda b, r, c, n: (0, blocks // extras, 0, 0)),
        pl.BlockSpec((width, occ), lambda b, r, c, n: (c[b + first], 0)),
    ]
    for e in range(extras):
        in_specs.append(pl.BlockSpec((width, occ), lambda b, r, c, n, e=e: (c[blocks + e], 0)))
    part = width // outs
    out = pl.pallas_call(
        functools.partial(half_body, first, blocks, extras, outs),
        grid_spec=pltpu.PrefetchScalarGridSpec(
            num_scalar_prefetch=3,
            grid=(count,),
            in_specs=in_specs,
            out_specs=[pl.BlockSpec((part, wide), lambda b, r, c, n: (b, 0))] * outs,
            scratch_shapes=[pltpu.VMEM((width, wide), F32)],
        ),
        out_shape=[jax.ShapeDtypeStruct((count * part, wide), BF16)] * outs,
        compiler_params=pltpu.CompilerParams(vmem_limit_bytes=LIMIT),
        cost_estimate=pl.CostEstimate(
            flops=4 * count * width * wide * width,
            bytes_accessed=2 * (count * (aux_dev * width * width + width * wide) + aux_dev * extras * width * width),
            transcendentals=0),
    )(rows, cols, live, tiles, tiles, *([orbitals] * (1 + extras)))
    return out


def mix_body(occ, weight, near, far, out):
    outs_q = out.shape[1] // occ
    ins_q = near.shape[1] // occ
    step = 16

    def chunk(c, carry):
        span = pl.ds(pl.multiple_of(c * step, step), step)
        sums = [None] * outs_q
        for k in range(2 * ins_q):
            ref, q = (near, k) if k < ins_q else (far, k - ins_q)
            x = ref[span, q * occ:(q + 1) * occ].astype(F32)
            for p in range(outs_q):
                term = x * weight[p, k]
                sums[p] = term if sums[p] is None else sums[p] + term
        for p in range(outs_q):
            out[span, p * occ:(p + 1) * occ] = sums[p].astype(out.dtype)
        return carry

    lax.fori_loop(0, near.shape[0] // step, chunk, 0)


def mix(weight, near, far, occ, dtype):
    rows, wide = near.shape
    return pl.pallas_call(
        functools.partial(mix_body, occ),
        in_specs=[pl.BlockSpec(memory_space=pltpu.SMEM)] + [pl.BlockSpec(memory_space=pltpu.VMEM)] * 2,
        out_specs=pl.BlockSpec(memory_space=pltpu.VMEM),
        out_shape=jax.ShapeDtypeStruct((rows, wide), dtype),
        compiler_params=pltpu.CompilerParams(vmem_limit_bytes=LIMIT),
        cost_estimate=pl.CostEstimate(
            flops=2 * rows * wide * weight.shape[1] * 100, bytes_accessed=8 * rows * wide, transcendentals=0),
    )(weight, near, far)


def product_body(places, *refs):
    pieces, right, send, near, own, left = refs[:4], refs[4], refs[5], refs[6], refs[7], refs[8]
    rows = pieces[0].shape[0]

    @pl.when(pl.program_id(0) == 0)
    def _():
        for k in range(4):
            left[pl.ds(pl.multiple_of(places[k] * rows, rows), rows), :] = pieces[k][...]

    product = lax.dot_general(
        left[...], right[...], (((1,), (1,)), ((), ())), preferred_element_type=F32)
    send[...] = product[:2 * rows].astype(BF16)
    near[...] = product[2 * rows:3 * rows]
    own[...] = product[3 * rows:]


def product_rows(places, pieces, right):
    rows, wide = pieces[0].shape
    count = right.shape[0]
    step = 512
    whole = pl.BlockSpec((rows, wide), lambda n, s: (0, 0))
    return pl.pallas_call(
        product_body,
        grid_spec=pltpu.PrefetchScalarGridSpec(
            num_scalar_prefetch=1,
            grid=(count // step,),
            in_specs=[whole] * 4 + [pl.BlockSpec((step, wide), lambda n, s: (n, 0))],
            out_specs=[
                pl.BlockSpec((2 * rows, step), lambda n, s: (0, n)),
                pl.BlockSpec((rows, step), lambda n, s: (0, n)),
                pl.BlockSpec((rows, step), lambda n, s: (0, n)),
            ],
            scratch_shapes=[pltpu.VMEM((4 * rows, wide), BF16)],
        ),
        out_shape=[
            jax.ShapeDtypeStruct((2 * rows, count), BF16),
            jax.ShapeDtypeStruct((rows, count), F32),
            jax.ShapeDtypeStruct((rows, count), F32),
        ],
        compiler_params=pltpu.CompilerParams(vmem_limit_bytes=LIMIT),
        cost_estimate=pl.CostEstimate(
            flops=8 * rows * wide * count, bytes_accessed=2 * wide * (count + 4 * rows), transcendentals=0),
    )(places, *pieces, right)


def swap(x, axis, distance):
    size = lax.axis_size(axis)
    return lax.ppermute(x, axis, [(i, i ^ distance) for i in range(size)])


def four_by_four(window, right, squared, aux_dev, occ):
    z, r = lax.axis_index("aux"), lax.axis_index("row")
    table = squared.reshape(4, aux_dev, 4, aux_dev)
    pick = lambda p, q: table[p, :, q, :]
    weights = [jnp.concatenate([pick(p, z), pick(p, z ^ 2)], axis=1) for p in (z ^ 1, z)]
    place = jnp.array([3, 0, 2, 1], jnp.int32)
    places = place[(r ^ jnp.arange(4, dtype=jnp.int32)) ^ z]
    results = []
    for x in window:
        far = swap(x, "aux", 2)
        message = swap(mix(weights[0], x, far, occ, BF16), "aux", 1)
        mine = mix(weights[1], x, far, occ, F32)
        g0 = (mine + message.astype(F32)).astype(BF16)
        g2 = swap(g0, "row", 2)
        g1 = swap(g0, "row", 1)
        g3 = swap(g2, "row", 1)
        send, near, own = product_rows(places, (g0, g1, g2, g3), right)
        rows = near.shape[0]
        came = swap(send, "aux", 1)
        passed = swap((near + came[rows:].astype(F32)).astype(BF16), "aux", 2)
        results.append(own + came[:rows].astype(F32) + passed.astype(F32))
    return jnp.concatenate(results, axis=0)


def any_mesh(window, right, squared, aux_dev, occ):
    rows = window.shape[0]
    aux = lax.axis_size("aux")
    gathered = lax.all_gather(window, "aux", axis=0, tiled=True).reshape(aux, rows, aux_dev, occ)
    own = lax.dynamic_slice_in_dim(squared, lax.axis_index("aux") * aux_dev, aux_dev, 0)
    own = own.reshape(aux_dev, aux, aux_dev)
    mixed = jnp.einsum("paq,amqi->mpi", own, gathered.astype(F32), precision=lax.Precision.HIGHEST)
    left = lax.all_gather(mixed.astype(BF16).reshape(rows, -1), "row", axis=0, tiled=True)
    product = lax.dot_general(left, right, (((1,), (1,)), ((), ())), preferred_element_type=F32)
    return lax.psum_scatter(product, "aux", scatter_dimension=0, tiled=True)


def shards(tensor_tiles, pair_rows, pair_cols, live_count, orbitals, metric):
    aux_dev, _, width, _ = tensor_tiles.shape
    basis, occ = orbitals.shape
    blocks = basis // (width * lax.axis_size("row"))
    shape44 = lax.axis_size("aux") == 4 and lax.axis_size("row") == 4
    squared = jnp.dot(metric.T, metric, preferred_element_type=F32)
    halves = functools.partial(
        half_rows, tensor_tiles, pair_rows[0], pair_cols[0], live_count[0], orbitals)
    window = halves(0, 1, HALVES if shape44 else 1)
    right, = halves(0, blocks, 1)
    if shape44:
        return four_by_four(window, right, squared, aux_dev, occ)
    return any_mesh(window[0], right, squared, aux_dev, occ)


def solution(mesh):
    return jax.shard_map(
        shards,
        mesh=mesh,
        in_specs=(
            P(("groups", "aux"), "row", None, None),
            P(("groups", "aux"), "row"),
            P(("groups", "aux"), "row"),
            P(("groups", "aux"), "row"),
            P(None, "groups"),
            P(),
        ),
        out_specs=P(("groups", "aux"), "row"),
        check_vma=False,
    )
```

```python
import functools

import jax
import jax.numpy as jnp
from jax import lax
from jax.experimental import pallas as pl
from jax.experimental.pallas import tpu as pltpu
from jax.sharding import PartitionSpec as P

KR = 128
HALVES = 2
LIMIT = 8 * 1024 * 1024
WHOLE = 60 * 1024 * 1024
F32 = jnp.float32
BF16 = jnp.bfloat16


def add_slot(acc, tile, orb, fresh):
    aux_dev, width, _ = tile.shape
    term = jnp.dot(tile.reshape(aux_dev * width, width), orb, preferred_element_type=F32)
    acc[...] = term if fresh else acc[...] + term


def store_block(acc, outs, row, aux_dev):
    occ = acc.shape[1]
    width = acc.shape[0] // aux_dev
    part = width // len(outs)
    for k, out in enumerate(outs):
        for q in range(aux_dev):
            first = q * width + k * part
            out[pl.ds(row, part), q * occ:(q + 1) * occ] = acc[first:first + part, :].astype(BF16)


def window_body(blocks, outs, rows, cols, live, tiles, orbitals, *rest):
    out_refs, tile, orb, acc, tile_sems, orb_sems = rest[:outs], *rest[outs:]
    aux_dev, slots, width, _ = tiles.shape

    def copies(k, slot):
        row = pl.multiple_of(cols[0, slot] * width, width)
        return (pltpu.make_async_copy(tiles.at[:, slot], tile.at[k], tile_sems.at[k]),
                pltpu.make_async_copy(orbitals.at[pl.ds(row, width)], orb.at[k], orb_sems.at[k]))

    def wanted(slot):
        return (rows[0, slot] == 0) & (slot < live[0, 0])

    for copy in copies(0, 0):
        copy.start()
    for slot in range(blocks, slots):
        @pl.when(wanted(slot))
        def _():
            for copy in copies(slot - blocks + 1, slot):
                copy.start()
    for copy in copies(0, 0):
        copy.wait()
    add_slot(acc, tile[0], orb[0], True)
    for slot in range(blocks, slots):
        @pl.when(wanted(slot))
        def _():
            k = slot - blocks + 1
            for copy in copies(k, slot):
                copy.wait()
            add_slot(acc, tile[k], orb[k], False)
    store_block(acc, out_refs, 0, aux_dev)


def window_rows(tiles, rows, cols, live, orbitals, outs):
    aux_dev, slots, width, _ = tiles.shape
    basis, occ = orbitals.shape
    blocks = basis // (width * lax.axis_size("row"))
    held = slots - blocks + 1
    smem, hbm = pl.BlockSpec(memory_space=pltpu.SMEM), pl.BlockSpec(memory_space=pltpu.HBM)
    return pl.pallas_call(
        functools.partial(window_body, blocks, outs),
        in_specs=[smem] * 3 + [hbm] * 2,
        out_specs=[pl.BlockSpec(memory_space=pltpu.VMEM)] * outs,
        out_shape=[jax.ShapeDtypeStruct((width // outs, aux_dev * occ), BF16)] * outs,
        scratch_shapes=[
            pltpu.VMEM((held, aux_dev, width, width), BF16),
            pltpu.VMEM((held, width, occ), BF16),
            pltpu.VMEM((aux_dev * width, occ), F32),
            pltpu.SemaphoreType.DMA((held,)),
            pltpu.SemaphoreType.DMA((held,)),
        ],
        compiler_params=pltpu.CompilerParams(vmem_limit_bytes=WHOLE),
        cost_estimate=pl.CostEstimate(
            flops=4 * aux_dev * width * width * occ, bytes_accessed=4 * aux_dev * width * width,
            transcendentals=0),
    )(rows, cols, live, tiles, orbitals)


def half_body(blocks, rows, cols, live, tiles, orbitals, weights, out, same, acc):
    same[...] = weights[...]
    aux_dev, slots, width, _ = tiles.shape

    def columns(slot):
        return orbitals[pl.ds(pl.multiple_of(cols[0, slot] * width, width), width), :]

    def block(b, carry):
        add_slot(acc, tiles[:, b], columns(b), True)

        def extra(slot, inner):
            @pl.when(rows[0, slot] == b)
            def _():
                add_slot(acc, tiles[:, slot], columns(slot), False)
            return inner

        lax.fori_loop(blocks, jnp.minimum(live[0, 0], slots), extra, 0)
        store_block(acc, [out], pl.multiple_of(b * width, width), aux_dev)
        return carry

    lax.fori_loop(0, blocks, block, 0)


def half_rows(tiles, rows, cols, live, orbitals, weights):
    aux_dev, slots, width, _ = tiles.shape
    basis, occ = orbitals.shape
    blocks = basis // (width * lax.axis_size("row"))
    wide = aux_dev * occ
    smem, vmem = pl.BlockSpec(memory_space=pltpu.SMEM), pl.BlockSpec(memory_space=pltpu.VMEM)
    return pl.pallas_call(
        functools.partial(half_body, blocks),
        in_specs=[smem] * 3 + [vmem] * 3,
        out_specs=[vmem] * 2,
        out_shape=[
            jax.ShapeDtypeStruct((blocks * width, wide), BF16),
            jax.ShapeDtypeStruct(weights.shape, weights.dtype),
        ],
        scratch_shapes=[pltpu.VMEM((aux_dev * width, occ), F32)],
        compiler_params=pltpu.CompilerParams(vmem_limit_bytes=LIMIT),
        cost_estimate=pl.CostEstimate(
            flops=4 * slots * aux_dev * width * width * occ,
            bytes_accessed=2 * (slots * aux_dev * width * width + basis * occ + blocks * width * wide),
            transcendentals=0),
    )(rows, cols, live, tiles, orbitals, weights)


def mix_body(occ, which, weight, near, far, out):
    outs_q = out.shape[1] // occ
    ins_q = near.shape[1] // occ
    step = 16

    def chunk(c, carry):
        span = pl.ds(pl.multiple_of(c * step, step), step)
        sums = [None] * outs_q
        for k in range(2 * ins_q):
            ref, q = (near, k) if k < ins_q else (far, k - ins_q)
            x = ref[span, q * occ:(q + 1) * occ].astype(F32)
            for p in range(outs_q):
                term = x * weight[which, p, k]
                sums[p] = term if sums[p] is None else sums[p] + term
        for p in range(outs_q):
            out[span, p * occ:(p + 1) * occ] = sums[p].astype(out.dtype)
        return carry

    lax.fori_loop(0, near.shape[0] // step, chunk, 0)


def mix(weight, which, near, far, occ, dtype):
    rows, wide = near.shape
    return pl.pallas_call(
        functools.partial(mix_body, occ, which),
        in_specs=[pl.BlockSpec(memory_space=pltpu.SMEM)] + [pl.BlockSpec(memory_space=pltpu.VMEM)] * 2,
        out_specs=pl.BlockSpec(memory_space=pltpu.VMEM),
        out_shape=jax.ShapeDtypeStruct((rows, wide), dtype),
        compiler_params=pltpu.CompilerParams(vmem_limit_bytes=LIMIT),
        cost_estimate=pl.CostEstimate(
            flops=2 * rows * wide * weight.shape[2], bytes_accessed=8 * rows * wide, transcendentals=0),
    )(weight, near, far)


def product_body(flag, even, odd, right, send, keep, left):
    rows, count = even.shape[0], right.shape[0]
    step = 512
    for k, piece in ((0, even), (1, odd)):
        place = jnp.where(flag[0] == k, rows, 0)
        left[pl.ds(pl.multiple_of(place, rows), rows), :] = piece[...]

    for n in range(count // step):
        product = lax.dot_general(
            left[...], right[n * step:(n + 1) * step, :], (((1,), (1,)), ((), ())),
            preferred_element_type=F32)
        send[:, n * step:(n + 1) * step] = product[:rows].astype(BF16)
        keep[:, n * step:(n + 1) * step] = product[rows:]


def product_rows(flag, even, odd, right):
    rows, wide = even.shape
    count = right.shape[0]
    vmem = pl.BlockSpec(memory_space=pltpu.VMEM)
    return pl.pallas_call(
        product_body,
        in_specs=[pl.BlockSpec(memory_space=pltpu.SMEM)] + [vmem] * 3,
        out_specs=[vmem] * 2,
        scratch_shapes=[pltpu.VMEM((2 * rows, wide), BF16)],
        out_shape=[
            jax.ShapeDtypeStruct((rows, count), BF16),
            jax.ShapeDtypeStruct((rows, count), F32),
        ],
        compiler_params=pltpu.CompilerParams(vmem_limit_bytes=LIMIT),
        cost_estimate=pl.CostEstimate(
            flops=4 * rows * wide * count, bytes_accessed=2 * wide * (count + 2 * rows), transcendentals=0),
    )(flag, even, odd, right)


def swap(x, axis, distance):
    size = lax.axis_size(axis)
    return lax.ppermute(x, axis, [(i, i ^ distance) for i in range(size)])


def forward(x, late):
    pairs = []
    for z in range(4):
        for r in range(4):
            if ((z ^ r) & 2 == 0) == late:
                pairs.append((z * 4 + r, (z ^ 2) * 4 + r))
    return lax.ppermute(x, ("aux", "row"), pairs)


def four_by_four(args, squared):
    aux_dev, occ = args[0].shape[0], args[-1].shape[1]
    z, r = lax.axis_index("aux"), lax.axis_index("row")
    table = squared.reshape(4, aux_dev, 4, aux_dev)
    pick = lambda p, q: table[p, :, q, :]
    weights = jnp.stack([jnp.concatenate([pick(p, z), pick(p, z ^ 2)], axis=1) for p in (z ^ 1, z)])
    window = window_rows(*args, HALVES)
    flag = jnp.reshape((r ^ z) & 1, (1,))
    first_own = ((r ^ z) & 2) == 0
    fars = [swap(x, "aux", 2) for x in window]
    right, weights = half_rows(*args, weights)
    pieces = []
    for x, far in zip(window, fars):
        message = swap(mix(weights, 0, x, far, occ, BF16), "aux", 1)
        mine = mix(weights, 1, x, far, occ, F32)
        g0 = (mine + message.astype(F32)).astype(BF16)
        g1 = swap(g0, "row", 1)
        g2 = swap(g0, "row", 2)
        g3 = swap(g2, "row", 1)
        pieces.append(((g0, g1), (g2, g3)))
    sums = [[], []]
    for late in (0, 1):
        for piece in pieces:
            send, keep = product_rows(flag, *piece[late], right)
            came = swap(send, "aux", 1)
            total = keep + came.astype(F32)
            passed = forward(total.astype(BF16), late == 1)
            sums[late].append((total, passed))
    results = [
        jnp.where(first_own, early, late) + passed_early.astype(F32) + passed_late.astype(F32)
        for (early, passed_early), (late, passed_late) in zip(*sums)
    ]
    return jnp.concatenate(results, axis=0)


def any_mesh(args, squared):
    aux_dev, occ = args[0].shape[0], args[-1].shape[1]
    window, = window_rows(*args, 1)
    right, squared = half_rows(*args, squared)
    rows = window.shape[0]
    aux = lax.axis_size("aux")
    gathered = lax.all_gather(window, "aux", axis=0, tiled=True).reshape(aux, rows, aux_dev, occ)
    own = lax.dynamic_slice_in_dim(squared, lax.axis_index("aux") * aux_dev, aux_dev, 0)
    own = own.reshape(aux_dev, aux, aux_dev)
    mixed = jnp.einsum("paq,amqi->mpi", own, gathered.astype(F32), precision=lax.Precision.HIGHEST)
    left = lax.all_gather(mixed.astype(BF16).reshape(rows, -1), "row", axis=0, tiled=True)
    product = lax.dot_general(left, right, (((1,), (1,)), ((), ())), preferred_element_type=F32)
    return lax.psum_scatter(product, "aux", scatter_dimension=0, tiled=True)


def shards(tensor_tiles, pair_rows, pair_cols, live_count, orbitals, metric):
    squared = jnp.dot(metric.T, metric, preferred_element_type=F32)
    args = (tensor_tiles, pair_rows, pair_cols, live_count, orbitals)
    if lax.axis_size("aux") == 4 and lax.axis_size("row") == 4:
        return four_by_four(args, squared)
    return any_mesh(args, squared)


def solution(mesh):
    return jax.shard_map(
        shards,
        mesh=mesh,
        in_specs=(
            P(("groups", "aux"), "row", None, None),
            P(("groups", "aux"), "row"),
            P(("groups", "aux"), "row"),
            P(("groups", "aux"), "row"),
            P(None, "groups"),
            P(),
        ),
        out_specs=P(("groups", "aux"), "row"),
        check_vma=False,
    )
```

```python
import functools

import jax
import jax.numpy as jnp
from jax import lax
from jax.experimental import pallas as pl
from jax.experimental.pallas import tpu as pltpu
from jax.sharding import PartitionSpec as P

KR = 128
HALVES = 2
LIMIT = 8 * 1024 * 1024
WHOLE = 60 * 1024 * 1024
F32 = jnp.float32
BF16 = jnp.bfloat16


def add_slot(acc, tile, orb, fresh):
    aux_dev, width, _ = tile.shape
    term = jnp.dot(tile.reshape(aux_dev * width, width), orb, preferred_element_type=F32)
    acc[...] = term if fresh else acc[...] + term


def store_block(acc, outs, row, aux_dev):
    occ = acc.shape[1]
    width = acc.shape[0] // aux_dev
    part = width // len(outs)
    for k, out in enumerate(outs):
        for q in range(aux_dev):
            first = q * width + k * part
            out[pl.ds(row, part), q * occ:(q + 1) * occ] = acc[first:first + part, :].astype(BF16)


def window_body(blocks, outs, rows, cols, live, tiles, orbitals, *rest):
    out_refs, tile, orb, acc, tile_sems, orb_sems = rest[:outs], *rest[outs:]
    aux_dev, slots, width, _ = tiles.shape

    def copies(k, slot):
        row = pl.multiple_of(cols[0, slot] * width, width)
        return (pltpu.make_async_copy(tiles.at[:, slot], tile.at[k], tile_sems.at[k]),
                pltpu.make_async_copy(orbitals.at[pl.ds(row, width)], orb.at[k], orb_sems.at[k]))

    def wanted(slot):
        return (rows[0, slot] == 0) & (slot < live[0, 0])

    for copy in copies(0, 0):
        copy.start()
    for slot in range(blocks, slots):
        @pl.when(wanted(slot))
        def _():
            for copy in copies(slot - blocks + 1, slot):
                copy.start()
    for copy in copies(0, 0):
        copy.wait()
    add_slot(acc, tile[0], orb[0], True)
    for slot in range(blocks, slots):
        @pl.when(wanted(slot))
        def _():
            k = slot - blocks + 1
            for copy in copies(k, slot):
                copy.wait()
            add_slot(acc, tile[k], orb[k], False)
    store_block(acc, out_refs, 0, aux_dev)


def window_rows(tiles, rows, cols, live, orbitals, outs):
    aux_dev, slots, width, _ = tiles.shape
    basis, occ = orbitals.shape
    blocks = basis // (width * lax.axis_size("row"))
    held = slots - blocks + 1
    smem, hbm = pl.BlockSpec(memory_space=pltpu.SMEM), pl.BlockSpec(memory_space=pltpu.HBM)
    return pl.pallas_call(
        functools.partial(window_body, blocks, outs),
        in_specs=[smem] * 3 + [hbm] * 2,
        out_specs=[pl.BlockSpec(memory_space=pltpu.VMEM)] * outs,
        out_shape=[jax.ShapeDtypeStruct((width // outs, aux_dev * occ), BF16)] * outs,
        scratch_shapes=[
            pltpu.VMEM((held, aux_dev, width, width), BF16),
            pltpu.VMEM((held, width, occ), BF16),
            pltpu.VMEM((aux_dev * width, occ), F32),
            pltpu.SemaphoreType.DMA((held,)),
            pltpu.SemaphoreType.DMA((held,)),
        ],
        compiler_params=pltpu.CompilerParams(vmem_limit_bytes=WHOLE),
        cost_estimate=pl.CostEstimate(
            flops=4 * aux_dev * width * width * occ, bytes_accessed=4 * aux_dev * width * width,
            transcendentals=0),
    )(rows, cols, live, tiles, orbitals)


def half_body(blocks, rows, cols, live, tiles, orbitals, weights, out, same, acc):
    same[...] = weights[...]
    aux_dev, slots, width, _ = tiles.shape

    def columns(slot):
        return orbitals[pl.ds(pl.multiple_of(cols[0, slot] * width, width), width), :]

    def block(b, carry):
        add_slot(acc, tiles[:, b], columns(b), True)

        def extra(slot, inner):
            @pl.when(rows[0, slot] == b)
            def _():
                add_slot(acc, tiles[:, slot], columns(slot), False)
            return inner

        lax.fori_loop(blocks, jnp.minimum(live[0, 0], slots), extra, 0)
        store_block(acc, [out], pl.multiple_of(b * width, width), aux_dev)
        return carry

    lax.fori_loop(0, blocks, block, 0)


def half_rows(tiles, rows, cols, live, orbitals, weights):
    aux_dev, slots, width, _ = tiles.shape
    basis, occ = orbitals.shape
    blocks = basis // (width * lax.axis_size("row"))
    wide = aux_dev * occ
    smem, vmem = pl.BlockSpec(memory_space=pltpu.SMEM), pl.BlockSpec(memory_space=pltpu.VMEM)
    return pl.pallas_call(
        functools.partial(half_body, blocks),
        in_specs=[smem] * 3 + [vmem] * 3,
        out_specs=[vmem] * 2,
        out_shape=[
            jax.ShapeDtypeStruct((blocks * width, wide), BF16),
            jax.ShapeDtypeStruct(weights.shape, weights.dtype),
        ],
        scratch_shapes=[pltpu.VMEM((aux_dev * width, occ), F32)],
        compiler_params=pltpu.CompilerParams(vmem_limit_bytes=LIMIT),
        cost_estimate=pl.CostEstimate(
            flops=4 * slots * aux_dev * width * width * occ,
            bytes_accessed=2 * (slots * aux_dev * width * width + basis * occ + blocks * width * wide),
            transcendentals=0),
    )(rows, cols, live, tiles, orbitals, weights)


def mix_body(occ, which, weight, near, far, out):
    outs_q = out.shape[1] // occ
    ins_q = near.shape[1] // occ
    step = 16

    def chunk(c, carry):
        span = pl.ds(pl.multiple_of(c * step, step), step)
        sums = [None] * outs_q
        for k in range(2 * ins_q):
            ref, q = (near, k) if k < ins_q else (far, k - ins_q)
            x = ref[span, q * occ:(q + 1) * occ].astype(F32)
            for p in range(outs_q):
                term = x * weight[which, p, k]
                sums[p] = term if sums[p] is None else sums[p] + term
        for p in range(outs_q):
            out[span, p * occ:(p + 1) * occ] = sums[p].astype(out.dtype)
        return carry

    lax.fori_loop(0, near.shape[0] // step, chunk, 0)


def mix(weight, which, near, far, occ, dtype):
    rows, wide = near.shape
    return pl.pallas_call(
        functools.partial(mix_body, occ, which),
        in_specs=[pl.BlockSpec(memory_space=pltpu.SMEM)] + [pl.BlockSpec(memory_space=pltpu.VMEM)] * 2,
        out_specs=pl.BlockSpec(memory_space=pltpu.VMEM),
        out_shape=jax.ShapeDtypeStruct((rows, wide), dtype),
        compiler_params=pltpu.CompilerParams(vmem_limit_bytes=LIMIT),
        cost_estimate=pl.CostEstimate(
            flops=2 * rows * wide * weight.shape[2], bytes_accessed=8 * rows * wide, transcendentals=0),
    )(weight, near, far)


def product_body(flag, even, odd, right, send, keep, left):
    rows, count = even.shape[0], right.shape[0]
    step = 512
    for k, piece in ((0, even), (1, odd)):
        place = jnp.where(flag[0] == k, rows, 0)
        left[pl.ds(pl.multiple_of(place, rows), rows), :] = piece[...]

    for n in range(count // step):
        product = lax.dot_general(
            left[...], right[n * step:(n + 1) * step, :], (((1,), (1,)), ((), ())),
            preferred_element_type=F32)
        send[:, n * step:(n + 1) * step] = product[:rows].astype(BF16)
        keep[:, n * step:(n + 1) * step] = product[rows:]


def product_rows(flag, even, odd, right):
    rows, wide = even.shape
    count = right.shape[0]
    vmem = pl.BlockSpec(memory_space=pltpu.VMEM)
    return pl.pallas_call(
        product_body,
        in_specs=[pl.BlockSpec(memory_space=pltpu.SMEM)] + [vmem] * 3,
        out_specs=[vmem] * 2,
        scratch_shapes=[pltpu.VMEM((2 * rows, wide), BF16)],
        out_shape=[
            jax.ShapeDtypeStruct((rows, count), BF16),
            jax.ShapeDtypeStruct((rows, count), F32),
        ],
        compiler_params=pltpu.CompilerParams(vmem_limit_bytes=LIMIT),
        cost_estimate=pl.CostEstimate(
            flops=4 * rows * wide * count, bytes_accessed=2 * wide * (count + 2 * rows), transcendentals=0),
    )(flag, even, odd, right)


def swap(x, axis, distance):
    size = lax.axis_size(axis)
    return lax.ppermute(x, axis, [(i, i ^ distance) for i in range(size)])


def four_by_four(args, squared):
    aux_dev, occ = args[0].shape[0], args[-1].shape[1]
    z, r = lax.axis_index("aux"), lax.axis_index("row")
    table = squared.reshape(4, aux_dev, 4, aux_dev)
    pick = lambda p, q: table[p, :, q, :]
    weights = jnp.stack([jnp.concatenate([pick(p, z), pick(p, z ^ 2)], axis=1) for p in (z ^ 1, z)])
    window = window_rows(*args, HALVES)
    flag = jnp.reshape((r ^ z) & 1, (1,))
    first_own = ((r ^ z) & 2) == 0
    fars = [swap(x, "aux", 2) for x in window]
    right, weights = half_rows(*args, weights)
    pieces = []
    for x, far in zip(window, fars):
        message = swap(mix(weights, 0, x, far, occ, BF16), "aux", 1)
        mine = mix(weights, 1, x, far, occ, F32)
        g0 = (mine + message.astype(F32)).astype(BF16)
        g1 = swap(g0, "row", 1)
        g2 = swap(g0, "row", 2)
        g3 = swap(g2, "row", 1)
        pieces.append(((g0, g1), (g2, g3)))
    sums = [[], []]
    for late in (0, 1):
        for piece in pieces:
            send, keep = product_rows(flag, *piece[late], right)
            sums[late].append(keep + swap(send, "aux", 1).astype(F32))
    results = []
    for early, late in zip(*sums):
        passed = swap(jnp.where(first_own, late, early).astype(BF16), "aux", 2)
        results.append(jnp.where(first_own, early, late) + passed.astype(F32))
    return jnp.concatenate(results, axis=0)


def any_mesh(args, squared):
    aux_dev, occ = args[0].shape[0], args[-1].shape[1]
    window, = window_rows(*args, 1)
    right, squared = half_rows(*args, squared)
    rows = window.shape[0]
    aux = lax.axis_size("aux")
    gathered = lax.all_gather(window, "aux", axis=0, tiled=True).reshape(aux, rows, aux_dev, occ)
    own = lax.dynamic_slice_in_dim(squared, lax.axis_index("aux") * aux_dev, aux_dev, 0)
    own = own.reshape(aux_dev, aux, aux_dev)
    mixed = jnp.einsum("paq,amqi->mpi", own, gathered.astype(F32), precision=lax.Precision.HIGHEST)
    left = lax.all_gather(mixed.astype(BF16).reshape(rows, -1), "row", axis=0, tiled=True)
    product = lax.dot_general(left, right, (((1,), (1,)), ((), ())), preferred_element_type=F32)
    return lax.psum_scatter(product, "aux", scatter_dimension=0, tiled=True)


def shards(tensor_tiles, pair_rows, pair_cols, live_count, orbitals, metric):
    squared = jnp.dot(metric.T, metric, preferred_element_type=F32)
    args = (tensor_tiles, pair_rows, pair_cols, live_count, orbitals)
    if lax.axis_size("aux") == 4 and lax.axis_size("row") == 4:
        return four_by_four(args, squared)
    return any_mesh(args, squared)


def solution(mesh):
    return jax.shard_map(
        shards,
        mesh=mesh,
        in_specs=(
            P(("groups", "aux"), "row", None, None),
            P(("groups", "aux"), "row"),
            P(("groups", "aux"), "row"),
            P(("groups", "aux"), "row"),
            P(None, "groups"),
            P(),
        ),
        out_specs=P(("groups", "aux"), "row"),
        check_vma=False,
    )
```

```python
import functools

import jax
import jax.numpy as jnp
from jax import lax
from jax.experimental import pallas as pl
from jax.experimental.pallas import tpu as pltpu
from jax.sharding import PartitionSpec as P

KR = 128
HALVES = 2
LIMIT = 8 * 1024 * 1024
WHOLE = 60 * 1024 * 1024
F32 = jnp.float32
BF16 = jnp.bfloat16


def add_slot(acc, tile, orb, fresh):
    aux_dev, width, _ = tile.shape
    term = jnp.dot(tile.reshape(aux_dev * width, width), orb, preferred_element_type=F32)
    acc[...] = term if fresh else acc[...] + term


def store_block(acc, outs, row, aux_dev):
    occ = acc.shape[1]
    width = acc.shape[0] // aux_dev
    part = width // len(outs)
    for k, out in enumerate(outs):
        for q in range(aux_dev):
            first = q * width + k * part
            out[pl.ds(row, part), q * occ:(q + 1) * occ] = acc[first:first + part, :].astype(BF16)


def window_body(blocks, outs, rows, cols, live, tiles, orbitals, *rest):
    out_refs, tile, orb, acc, tile_sems, orb_sems = rest[:outs], *rest[outs:]
    aux_dev, slots, width, _ = tiles.shape

    def copies(k, slot):
        row = pl.multiple_of(cols[0, slot] * width, width)
        return (pltpu.make_async_copy(tiles.at[:, slot], tile.at[k], tile_sems.at[k]),
                pltpu.make_async_copy(orbitals.at[pl.ds(row, width)], orb.at[k], orb_sems.at[k]))

    def wanted(slot):
        return (rows[0, slot] == 0) & (slot < live[0, 0])

    for copy in copies(0, 0):
        copy.start()
    for slot in range(blocks, slots):
        @pl.when(wanted(slot))
        def _():
            for copy in copies(slot - blocks + 1, slot):
                copy.start()
    for copy in copies(0, 0):
        copy.wait()
    add_slot(acc, tile[0], orb[0], True)
    for slot in range(blocks, slots):
        @pl.when(wanted(slot))
        def _():
            k = slot - blocks + 1
            for copy in copies(k, slot):
                copy.wait()
            add_slot(acc, tile[k], orb[k], False)
    store_block(acc, out_refs, 0, aux_dev)


def window_rows(tiles, rows, cols, live, orbitals, outs):
    aux_dev, slots, width, _ = tiles.shape
    basis, occ = orbitals.shape
    blocks = basis // (width * lax.axis_size("row"))
    held = slots - blocks + 1
    smem, hbm = pl.BlockSpec(memory_space=pltpu.SMEM), pl.BlockSpec(memory_space=pltpu.HBM)
    return pl.pallas_call(
        functools.partial(window_body, blocks, outs),
        in_specs=[smem] * 3 + [hbm] * 2,
        out_specs=[pl.BlockSpec(memory_space=pltpu.VMEM)] * outs,
        out_shape=[jax.ShapeDtypeStruct((width // outs, aux_dev * occ), BF16)] * outs,
        scratch_shapes=[
            pltpu.VMEM((held, aux_dev, width, width), BF16),
            pltpu.VMEM((held, width, occ), BF16),
            pltpu.VMEM((aux_dev * width, occ), F32),
            pltpu.SemaphoreType.DMA((held,)),
            pltpu.SemaphoreType.DMA((held,)),
        ],
        compiler_params=pltpu.CompilerParams(vmem_limit_bytes=WHOLE),
        cost_estimate=pl.CostEstimate(flops=1_000_000_000, bytes_accessed=3_333_333, transcendentals=0),
    )(rows, cols, live, tiles, orbitals)


def half_body(blocks, rows, cols, live, tiles, orbitals, weights, out, same, acc):
    same[...] = weights[...]
    aux_dev, slots, width, _ = tiles.shape

    def columns(slot):
        return orbitals[pl.ds(pl.multiple_of(cols[0, slot] * width, width), width), :]

    def block(b, carry):
        add_slot(acc, tiles[:, b], columns(b), True)

        def extra(slot, inner):
            @pl.when(rows[0, slot] == b)
            def _():
                add_slot(acc, tiles[:, slot], columns(slot), False)
            return inner

        lax.fori_loop(blocks, jnp.minimum(live[0, 0], slots), extra, 0)
        store_block(acc, [out], pl.multiple_of(b * width, width), aux_dev)
        return carry

    lax.fori_loop(0, blocks, block, 0)


def half_rows(tiles, rows, cols, live, orbitals, weights):
    aux_dev, slots, width, _ = tiles.shape
    basis, occ = orbitals.shape
    blocks = basis // (width * lax.axis_size("row"))
    wide = aux_dev * occ
    smem, vmem = pl.BlockSpec(memory_space=pltpu.SMEM), pl.BlockSpec(memory_space=pltpu.VMEM)
    return pl.pallas_call(
        functools.partial(half_body, blocks),
        in_specs=[smem] * 3 + [vmem] * 3,
        out_specs=[vmem] * 2,
        out_shape=[
            jax.ShapeDtypeStruct((blocks * width, wide), BF16),
            jax.ShapeDtypeStruct(weights.shape, weights.dtype),
        ],
        scratch_shapes=[pltpu.VMEM((aux_dev * width, occ), F32)],
        compiler_params=pltpu.CompilerParams(vmem_limit_bytes=LIMIT),
        cost_estimate=pl.CostEstimate(flops=20_000_000_000, bytes_accessed=66_666_666, transcendentals=0),
    )(rows, cols, live, tiles, orbitals, weights)


def mix_body(occ, which, weight, near, far, out):
    outs_q = out.shape[1] // occ
    ins_q = near.shape[1] // occ
    step = 16

    def chunk(c, carry):
        span = pl.ds(pl.multiple_of(c * step, step), step)
        sums = [None] * outs_q
        for k in range(2 * ins_q):
            ref, q = (near, k) if k < ins_q else (far, k - ins_q)
            x = ref[span, q * occ:(q + 1) * occ].astype(F32)
            for p in range(outs_q):
                term = x * weight[which, p, k]
                sums[p] = term if sums[p] is None else sums[p] + term
        for p in range(outs_q):
            out[span, p * occ:(p + 1) * occ] = sums[p].astype(out.dtype)
        return carry

    lax.fori_loop(0, near.shape[0] // step, chunk, 0)


def mix(weight, which, near, far, occ, dtype):
    rows, wide = near.shape
    return pl.pallas_call(
        functools.partial(mix_body, occ, which),
        in_specs=[pl.BlockSpec(memory_space=pltpu.SMEM)] + [pl.BlockSpec(memory_space=pltpu.VMEM)] * 2,
        out_specs=pl.BlockSpec(memory_space=pltpu.VMEM),
        out_shape=jax.ShapeDtypeStruct((rows, wide), dtype),
        compiler_params=pltpu.CompilerParams(vmem_limit_bytes=LIMIT),
        cost_estimate=pl.CostEstimate(flops=2_000_000_000, bytes_accessed=6_666_666, transcendentals=0),
    )(weight, near, far)


def product_body(flag, even, odd, right, send, keep, left):
    rows, count = even.shape[0], right.shape[0]
    step = 512
    for k, piece in ((0, even), (1, odd)):
        place = jnp.where(flag[0] == k, rows, 0)
        left[pl.ds(pl.multiple_of(place, rows), rows), :] = piece[...]

    for n in range(count // step):
        product = lax.dot_general(
            left[...], right[n * step:(n + 1) * step, :], (((1,), (1,)), ((), ())),
            preferred_element_type=F32)
        send[:, n * step:(n + 1) * step] = product[:rows].astype(BF16)
        keep[:, n * step:(n + 1) * step] = product[rows:]


def product_rows(flag, even, odd, right):
    rows, wide = even.shape
    count = right.shape[0]
    vmem = pl.BlockSpec(memory_space=pltpu.VMEM)
    return pl.pallas_call(
        product_body,
        in_specs=[pl.BlockSpec(memory_space=pltpu.SMEM)] + [vmem] * 3,
        out_specs=[vmem] * 2,
        scratch_shapes=[pltpu.VMEM((2 * rows, wide), BF16)],
        out_shape=[
            jax.ShapeDtypeStruct((rows, count), BF16),
            jax.ShapeDtypeStruct((rows, count), F32),
        ],
        compiler_params=pltpu.CompilerParams(vmem_limit_bytes=LIMIT),
        cost_estimate=pl.CostEstimate(flops=3_000_000_000, bytes_accessed=10_000_000, transcendentals=0),
    )(flag, even, odd, right)


def swap(x, axis, distance):
    size = lax.axis_size(axis)
    return lax.ppermute(x, axis, [(i, i ^ distance) for i in range(size)])


def four_by_four(args, squared):
    aux_dev, occ = args[0].shape[0], args[-1].shape[1]
    z, r = lax.axis_index("aux"), lax.axis_index("row")
    table = squared.reshape(4, aux_dev, 4, aux_dev)
    pick = lambda p, q: table[p, :, q, :]
    weights = jnp.stack([jnp.concatenate([pick(p, z), pick(p, z ^ 2)], axis=1) for p in (z ^ 1, z)])
    window = window_rows(*args, HALVES)
    flag = jnp.reshape((r ^ z) & 1, (1,))
    first_own = ((r ^ z) & 2) == 0
    fars = [swap(x, "aux", 2) for x in window]
    right, weights = half_rows(*args, weights)
    pieces, sums, ready = [], [[], []], None
    for x, far in zip(window, fars):
        message = swap(mix(weights, 0, x, far, occ, BF16), "aux", 1)
        mine = mix(weights, 1, x, far, occ, F32)
        g0 = (mine + message.astype(F32)).astype(BF16)
        g1 = swap(g0, "row", 1)
        pieces.append(swap(g0, "row", 2))
        send, ready = product_rows(flag, g0, g1, right)
        sums[0].append(ready)
        sums[1].append(swap(send, "aux", 1))
    sums[0] = [keep + came.astype(F32) for keep, came in zip(*sums)]
    sums[1] = []
    for g2 in pieces:
        send, keep = product_rows(flag, g2, swap(g2, "row", 1), right)
        sums[1].append(keep + swap(send, "aux", 1).astype(F32))
    results = []
    for early, late in zip(*sums):
        passed = swap(jnp.where(first_own, late, early).astype(BF16), "aux", 2)
        results.append(jnp.where(first_own, early, late) + passed.astype(F32))
    return jnp.concatenate(results, axis=0)


def any_mesh(args, squared):
    aux_dev, occ = args[0].shape[0], args[-1].shape[1]
    window, = window_rows(*args, 1)
    right, squared = half_rows(*args, squared)
    rows = window.shape[0]
    aux = lax.axis_size("aux")
    gathered = lax.all_gather(window, "aux", axis=0, tiled=True).reshape(aux, rows, aux_dev, occ)
    own = lax.dynamic_slice_in_dim(squared, lax.axis_index("aux") * aux_dev, aux_dev, 0)
    own = own.reshape(aux_dev, aux, aux_dev)
    mixed = jnp.einsum("paq,amqi->mpi", own, gathered.astype(F32), precision=lax.Precision.HIGHEST)
    left = lax.all_gather(mixed.astype(BF16).reshape(rows, -1), "row", axis=0, tiled=True)
    product = lax.dot_general(left, right, (((1,), (1,)), ((), ())), preferred_element_type=F32)
    return lax.psum_scatter(product, "aux", scatter_dimension=0, tiled=True)


def shards(tensor_tiles, pair_rows, pair_cols, live_count, orbitals, metric):
    squared = jnp.dot(metric.T, metric, preferred_element_type=F32)
    args = (tensor_tiles, pair_rows, pair_cols, live_count, orbitals)
    if lax.axis_size("aux") == 4 and lax.axis_size("row") == 4:
        return four_by_four(args, squared)
    return any_mesh(args, squared)


def solution(mesh):
    return jax.shard_map(
        shards,
        mesh=mesh,
        in_specs=(
            P(("groups", "aux"), "row", None, None),
            P(("groups", "aux"), "row"),
            P(("groups", "aux"), "row"),
            P(("groups", "aux"), "row"),
            P(None, "groups"),
            P(),
        ),
        out_specs=P(("groups", "aux"), "row"),
        check_vma=False,
    )
```

```python
import functools

import jax
import jax.numpy as jnp
from jax import lax
from jax.experimental import pallas as pl
from jax.experimental.pallas import tpu as pltpu
from jax.sharding import PartitionSpec as P

KR = 128
HALVES = (48, 48, 32)
LIMIT = 8 * 1024 * 1024
MOST = 50 * 1024 * 1024
WHOLE = 60 * 1024 * 1024
F32 = jnp.float32
BF16 = jnp.bfloat16


def add_slot(acc, tile, orb, fresh):
    aux_dev, width, _ = tile.shape
    term = jnp.dot(tile.reshape(aux_dev * width, width), orb, preferred_element_type=F32)
    acc[...] = term if fresh else acc[...] + term


def store_block(acc, outs, row, aux_dev):
    occ = acc.shape[1]
    width = acc.shape[0] // aux_dev
    begin = 0
    for out in outs:
        part = min(out.shape[0], width)
        for q in range(aux_dev):
            first = q * width + begin
            out[pl.ds(row, part), q * occ:(q + 1) * occ] = acc[first:first + part, :].astype(BF16)
        begin += part


def window_body(blocks, outs, rows, cols, live, tiles, orbitals, *rest):
    out_refs, tile, orb, acc, tile_sems, orb_sems = rest[:outs], *rest[outs:]
    aux_dev, slots, width, _ = tiles.shape

    def copies(k, slot):
        row = pl.multiple_of(cols[0, slot] * width, width)
        return (pltpu.make_async_copy(tiles.at[:, slot], tile.at[k], tile_sems.at[k]),
                pltpu.make_async_copy(orbitals.at[pl.ds(row, width)], orb.at[k], orb_sems.at[k]))

    count = jnp.max(live[...])

    def wanted(slot):
        return (rows[0, slot] == 0) & (slot < count)

    for copy in copies(0, 0):
        copy.start()
    for slot in range(blocks, slots):
        @pl.when(wanted(slot))
        def _():
            for copy in copies(slot - blocks + 1, slot):
                copy.start()
    for copy in copies(0, 0):
        copy.wait()
    add_slot(acc, tile[0], orb[0], True)
    for slot in range(blocks, slots):
        @pl.when(wanted(slot))
        def _():
            k = slot - blocks + 1
            for copy in copies(k, slot):
                copy.wait()
            add_slot(acc, tile[k], orb[k], False)
    store_block(acc, out_refs, 0, aux_dev)


def window_rows(tiles, rows, cols, live, orbitals, outs):
    aux_dev, slots, width, _ = tiles.shape
    basis, occ = orbitals.shape
    blocks = basis // (width * lax.axis_size("row"))
    held = slots - blocks + 1
    smem, hbm = pl.BlockSpec(memory_space=pltpu.SMEM), pl.BlockSpec(memory_space=pltpu.HBM)
    vmem = pl.BlockSpec(memory_space=pltpu.VMEM)
    return pl.pallas_call(
        functools.partial(window_body, blocks, len(outs)),
        in_specs=[smem, smem, vmem] + [hbm] * 2,
        out_specs=[pl.BlockSpec(memory_space=pltpu.VMEM)] * len(outs),
        out_shape=[jax.ShapeDtypeStruct((part, aux_dev * occ), BF16) for part in outs],
        scratch_shapes=[
            pltpu.VMEM((held, aux_dev, width, width), BF16),
            pltpu.VMEM((held, width, occ), BF16),
            pltpu.VMEM((aux_dev * width, occ), F32),
            pltpu.SemaphoreType.DMA((held,)),
            pltpu.SemaphoreType.DMA((held,)),
        ],
        compiler_params=pltpu.CompilerParams(vmem_limit_bytes=WHOLE),
        cost_estimate=pl.CostEstimate(flops=1_000_000_000, bytes_accessed=3_333_333, transcendentals=0),
    )(rows, cols, live, tiles, orbitals)


def half_body(blocks, rows, cols, live, tiles, orbitals, weights, out, same,
              tile, orb, acc, tile_sems, orb_sems):
    aux_dev, slots, width, _ = tiles.shape
    occ = orbitals.shape[1]
    count = jnp.minimum(jnp.max(live[...]), slots)

    def copies(slot):
        row = pl.multiple_of(cols[0, slot] * width, width)
        return (pltpu.make_async_copy(tiles.at[:, slot], tile.at[slot], tile_sems.at[slot]),
                pltpu.make_async_copy(orbitals.at[pl.ds(row, width)], orb.at[slot], orb_sems.at[slot]))

    def start(slot, carry):
        for copy in copies(slot):
            copy.start()
        return carry

    def finish(slot):
        for copy in copies(slot):
            copy.wait()

    lax.fori_loop(0, 4, start, 0)
    lax.fori_loop(blocks, count, start, 0)
    lax.fori_loop(4, blocks, start, 0)
    same[...] = weights[...]

    def block(b, carry):
        finish(b)
        add_slot(acc, tile[b], orb[b], True)

        def extra(slot, inner):
            @pl.when(rows[0, slot] == b)
            def _():
                finish(slot)
                add_slot(acc, tile[slot], orb[slot], False)
            return inner

        lax.fori_loop(blocks, count, extra, 0)
        row = pl.multiple_of(b * width, width)
        store_block(acc, [out], row, aux_dev)
        return carry

    lax.fori_loop(0, blocks, block, 0)


def half_rows(tiles, rows, cols, live, orbitals, weights):
    aux_dev, slots, width, _ = tiles.shape
    basis, occ = orbitals.shape
    blocks = basis // (width * lax.axis_size("row"))
    wide = aux_dev * occ
    smem, hbm = pl.BlockSpec(memory_space=pltpu.SMEM), pl.BlockSpec(memory_space=pltpu.HBM)
    vmem = pl.BlockSpec(memory_space=pltpu.VMEM)
    return pl.pallas_call(
        functools.partial(half_body, blocks),
        in_specs=[smem, smem, vmem] + [hbm] * 2 + [vmem],
        out_specs=[vmem] * 2,
        out_shape=[
            jax.ShapeDtypeStruct((blocks * width, wide), BF16),
            jax.ShapeDtypeStruct(weights.shape, weights.dtype),
        ],
        scratch_shapes=[
            pltpu.VMEM((slots, aux_dev, width, width), BF16),
            pltpu.VMEM((slots, width, occ), BF16),
            pltpu.VMEM((aux_dev * width, occ), F32),
            pltpu.SemaphoreType.DMA((slots,)),
            pltpu.SemaphoreType.DMA((slots,)),
        ],
        compiler_params=pltpu.CompilerParams(vmem_limit_bytes=MOST),
        cost_estimate=pl.CostEstimate(flops=20_000_000_000, bytes_accessed=66_666_666, transcendentals=0),
    )(rows, cols, live, tiles, orbitals, weights)


def mix_body(occ, which, weight, near, far, out):
    outs_q = out.shape[1] // occ
    ins_q = near.shape[1] // occ
    step = 16

    def chunk(c, carry):
        span = pl.ds(pl.multiple_of(c * step, step), step)
        sums = [None] * outs_q
        for k in range(2 * ins_q):
            ref, q = (near, k) if k < ins_q else (far, k - ins_q)
            x = ref[span, q * occ:(q + 1) * occ].astype(F32)
            for p in range(outs_q):
                term = x * weight[which, p, k]
                sums[p] = term if sums[p] is None else sums[p] + term
        for p in range(outs_q):
            out[span, p * occ:(p + 1) * occ] = sums[p].astype(out.dtype)
        return carry

    lax.fori_loop(0, near.shape[0] // step, chunk, 0)


def mix(weight, which, near, far, occ, dtype, flops):
    rows, wide = near.shape
    return pl.pallas_call(
        functools.partial(mix_body, occ, which),
        in_specs=[pl.BlockSpec(memory_space=pltpu.SMEM)] + [pl.BlockSpec(memory_space=pltpu.VMEM)] * 2,
        out_specs=pl.BlockSpec(memory_space=pltpu.VMEM),
        out_shape=jax.ShapeDtypeStruct((rows, wide), dtype),
        compiler_params=pltpu.CompilerParams(vmem_limit_bytes=LIMIT),
        cost_estimate=pl.CostEstimate(flops=flops, bytes_accessed=flops // 300, transcendentals=0),
    )(weight, near, far)


def product_body(flag, even, odd, right, *rest):
    sends, keep, left = rest[:-2], rest[-2], rest[-1]
    rows, count = even.shape[0], right.shape[0]
    step = 512
    for k, piece in ((0, even), (1, odd)):
        place = jnp.where(flag[0] == k, rows, 0)
        left[pl.ds(pl.multiple_of(place, rows), rows), :] = piece[...]

    for n in range(count // step):
        product = lax.dot_general(
            left[...], right[n * step:(n + 1) * step, :], (((1,), (1,)), ((), ())),
            preferred_element_type=F32)
        part = count // len(sends)
        send, first = sends[n * step // part], n * step % part
        send[:, first:first + step] = product[:rows].astype(BF16)
        keep[:, n * step:(n + 1) * step] = product[rows:]


def product_rows(flag, even, odd, right, parts, flops):
    rows, wide = even.shape
    count = right.shape[0]
    vmem = pl.BlockSpec(memory_space=pltpu.VMEM)
    *sends, keep = pl.pallas_call(
        product_body,
        in_specs=[pl.BlockSpec(memory_space=pltpu.SMEM)] + [vmem] * 3,
        out_specs=[vmem] * (parts + 1),
        scratch_shapes=[pltpu.VMEM((2 * rows, wide), BF16)],
        out_shape=[jax.ShapeDtypeStruct((rows, count // parts), BF16)] * parts + [
            jax.ShapeDtypeStruct((rows, count), F32)],
        compiler_params=pltpu.CompilerParams(vmem_limit_bytes=LIMIT),
        cost_estimate=pl.CostEstimate(flops=flops, bytes_accessed=flops // 300, transcendentals=0),
    )(flag, even, odd, right)
    return sends, keep


def swap(x, axis, distance):
    size = lax.axis_size(axis)
    return lax.ppermute(x, axis, [(i, i ^ distance) for i in range(size)])


def four_by_four(args, squared):
    aux_dev, occ = args[0].shape[0], args[-1].shape[1]
    z, r = lax.axis_index("aux"), lax.axis_index("row")
    table = squared.reshape(4, aux_dev, 4, aux_dev)
    pick = lambda p, q: table[p, :, q, :]
    weights = jnp.stack([jnp.concatenate([pick(p, z), pick(p, z ^ 2)], axis=1) for p in (z ^ 1, z)])
    flag = jnp.reshape((r ^ z) & 1, (1,))
    first_own = ((r ^ z) & 2) == 0
    window = window_rows(*args, HALVES)
    right, weights = half_rows(*args, weights)
    fars = [swap(x, "aux", 2) for x in window]
    pieces, sums = [], []
    for x, far in zip(window, fars):
        message = swap(mix(weights, 0, x, far, occ, BF16, 2_000_000_000), "aux", 1)
        mine = mix(weights, 1, x, far, occ, F32, 2_000_000_000)
        g0 = (mine + message.astype(F32)).astype(BF16)
        g1 = swap(g0, "row", 1)
        pieces.append(swap(g0, "row", 2))
        sends, keep = product_rows(flag, g0, g1, right, 1, 3_000_000_000)
        got = [swap(send, "aux", 1).astype(F32) for send in sends]
        sums.append([keep + (got[0] if len(got) == 1 else jnp.concatenate(got, axis=1))])
    for g2, total, parts in zip(pieces, sums, (1,) * len(sums)):
        sends, keep = product_rows(flag, g2, swap(g2, "row", 1), right, parts, 3_000_000_000)
        total.append((keep, [swap(send, "aux", 1) for send in sends]))
    results = []
    for early, (keep, came) in sums:
        parts, step = [], keep.shape[1] // len(came)
        for k, got in enumerate(came):
            span = slice(k * step, (k + 1) * step)
            late = keep[:, span] + got.astype(F32)
            passed = swap(jnp.where(first_own, late, early[:, span]).astype(BF16), "aux", 2)
            parts.append(jnp.where(first_own, early[:, span], late) + passed.astype(F32))
        results.append(parts[0] if len(parts) == 1 else jnp.concatenate(parts, axis=1))
    return jnp.concatenate(results, axis=0)


def any_mesh(args, squared):
    aux_dev, occ = args[0].shape[0], args[-1].shape[1]
    right, squared = half_rows(*args, squared)
    window = right[:KR]
    rows = window.shape[0]
    aux = lax.axis_size("aux")
    gathered = lax.all_gather(window, "aux", axis=0, tiled=True).reshape(aux, rows, aux_dev, occ)
    own = lax.dynamic_slice_in_dim(squared, lax.axis_index("aux") * aux_dev, aux_dev, 0)
    own = own.reshape(aux_dev, aux, aux_dev)
    mixed = jnp.einsum("paq,amqi->mpi", own, gathered.astype(F32), precision=lax.Precision.HIGHEST)
    left = lax.all_gather(mixed.astype(BF16).reshape(rows, -1), "row", axis=0, tiled=True)
    product = lax.dot_general(left, right, (((1,), (1,)), ((), ())), preferred_element_type=F32)
    return lax.psum_scatter(product, "aux", scatter_dimension=0, tiled=True)


def shards(tensor_tiles, pair_rows, pair_cols, live_count, orbitals, metric):
    squared = jnp.dot(metric.T, metric, preferred_element_type=F32)
    args = (tensor_tiles, pair_rows, pair_cols, live_count, orbitals)
    if lax.axis_size("aux") == 4 and lax.axis_size("row") == 4:
        return four_by_four(args, squared)
    return any_mesh(args, squared)


def solution(mesh):
    return jax.shard_map(
        shards,
        mesh=mesh,
        in_specs=(
            P(("groups", "aux"), "row", None, None),
            P(("groups", "aux"), "row"),
            P(("groups", "aux"), "row"),
            P(("groups", "aux"), "row"),
            P(None, "groups"),
            P(),
        ),
        out_specs=P(("groups", "aux"), "row"),
        check_vma=False,
    )
```
